32 devices in a mesh: lat: 8 (over z, core), lon: 4 (over y, x).
Axes of the slice: x: 2, y: 2, z: 4, core: 2. Of those that a mesh axis runs over, the one named last changes fastest.
Arguments:
- east_wind: float32 [4, 4096, 8192], P(None, 'lat', 'lon'), may hold values from -6 to 6
- north_wind: float32 [4, 4096, 8192], P(None, 'lat', 'lon'), may hold values from -6 to 6
- pressure: float32 [4, 4096, 8192], P(None, 'lat', 'lon'), may hold values from -6 to 6
- sound_squared: float32 [4], replicated, may hold values from 0.5 to 2
- column_mass: float32 [4096, 8192], P('lat', 'lon'), may hold values from 0.5 to 1.5
- polar_rows: int32 [512], replicated, may hold values from 0 to 4095, as said below
- cutoffs: int32 [512], replicated, may hold values from 512 to 4095
Outputs:
- new_east: float32 [4, 4096, 8192], P(None, 'lat', 'lon')
- new_north: float32 [4, 4096, 8192], P(None, 'lat', 'lon')
- new_pressure: float32 [4, 4096, 8192], P(None, 'lat', 'lon')
The draws below stay inside these ranges and needn't reach their ends.
Inputs may be any that keep to these rules, and one draw needn't show every extreme that they name: `polar_rows`: distinct rows in ascending order, each poleward of 45 degrees (below 1024 or at least 3072); at most 256 of them lie in one band of 512 rows (rows b * 512 to (b + 1) * 512 - 1), and some band holds exactly 256.
All inputs are finite; a program needn't handle non-finite values.
Results may differ from the reference program's by a relative error of at most 0.00005.
Values sent between devices are 32-bit elements; how exact they have to be, the bound alone decides.
A program may use at most 320 MiB of HBM per device.

```python
import math
import jax
import jax.numpy as jnp

NLON = 8192
NLAT = 4096
LEVELS = 4
CLAT = 512
KSLOTS = 256
NPOLAR = 512


def draw_polar_rows(key, part):
    band_total = NLAT // CLAT
    polar_bands = band_total // 2
    midway = KSLOTS // 2
    spread = jax.random.randint(jax.random.fold_in(key, 11), (polar_bands // 2,), 0, midway + 1)
    spread = spread.at[0].set(midway)
    counts = jnp.stack([midway + spread, midway - spread], axis=1).reshape(polar_bands)
    band_keys = jax.random.split(jax.random.fold_in(key, 12), polar_bands)
    orders = jax.vmap(lambda one_key: jax.random.permutation(one_key, CLAT))(band_keys)
    chosen = orders < counts[:, None]
    polar_ids = jnp.arange(polar_bands, dtype=jnp.int32)
    band_ids = jnp.where(polar_ids < band_total // 4, polar_ids, polar_ids + band_total // 2)
    global_rows = band_ids[:, None] * CLAT + jnp.arange(CLAT, dtype=jnp.int32)[None, :]
    flags = jnp.zeros((NLAT,), jnp.int32).at[global_rows.reshape(-1)].set(chosen.reshape(-1).astype(jnp.int32))
    return jnp.nonzero(flags, size=NPOLAR)[0].astype(jnp.int32)


def with_ends(result, rng, low, largest):
    longest = result.shape.index(max(result.shape))
    spots = []
    for shift in (0, 1):
        where = [jax.random.randint(jax.random.fold_in(rng, axis), (), 0, length) for axis, length in enumerate(result.shape)]
        where[longest] = (where[longest] + shift) % result.shape[longest]
        spots.append(tuple(where))
    return result.at[spots[0]].set(low).at[spots[1]].set(largest)


def shard_levels(key, dims, shards, least, top_value):
    gain, own = 1.0, jax.random.fold_in(key, 6)
    for axis_at, shards_of in shards:
        draws = jnp.exp(jax.random.uniform(jax.random.fold_in(own, axis_at), (shards_of,), jnp.float32, least / len(shards), top_value / len(shards)))
        gain = gain * jnp.repeat(draws, dims[axis_at] // shards_of).reshape([-1 if axis == axis_at else 1 for axis in range(len(dims))])
    return gain


def bell_draw(own_key, extent, scale, reach, shards=(), kind=jnp.bfloat16):
    array = scale * jax.random.normal(own_key, extent, jnp.float32)
    if shards:
        array = array * shard_levels(own_key, extent, shards, -0.22, 0.18)
    return jnp.clip(array, -reach, reach).astype(kind)


def setup_inputs(seed: int = 0) -> dict:
    key_list = jax.random.split(jax.random.key(seed), 8)
    east_wind = bell_draw(key_list[0], (LEVELS, NLAT, NLON), 1.0, 6.0, ((1, 8), (2, 4)), jnp.float32)
    north_wind = bell_draw(key_list[1], (LEVELS, NLAT, NLON), 1.0, 6.0, ((1, 8), (2, 4)), jnp.float32)
    pressure = bell_draw(key_list[2], (LEVELS, NLAT, NLON), 1.0, 6.0, ((1, 8), (2, 4)), jnp.float32)
    sound_squared = jnp.clip(jnp.exp(jax.random.uniform(key_list[3], (LEVELS,), jnp.float32, math.log(0.5), math.log(2.0))), 0.5, 2.0)
    column_mass = jnp.clip(0.5 + 1.0 * jax.random.uniform(key_list[4], (NLAT, NLON), jnp.float32) ** shard_levels(key_list[4], (NLAT, NLON), ((0, 8), (1, 4)), -0.2, 0.2), 0.5, 1.5)
    polar_rows = draw_polar_rows(jax.random.fold_in(key_list[7], 71), 0)
    cutoffs = with_ends(jax.random.randint(key_list[6], (NPOLAR,), NLON // 16, NLON // 2), jax.random.fold_in(key_list[6], 1), NLON // 16, (NLON // 2) - 1).astype(jnp.int32)
    return {"east_wind": east_wind, "north_wind": north_wind, "pressure": pressure, "sound_squared": sound_squared, "column_mass": column_mass, "polar_rows": polar_rows, "cutoffs": cutoffs}


def latitude_terms(global_rows, total_rows):
    latitude = (-0.5 + (global_rows.astype(jnp.float32) + 0.5) / total_rows) * jnp.pi
    cosine = jnp.cos(latitude)
    courant = 0.3 * jnp.minimum(1.0 / cosine, 2.0)
    return cosine, courant


def reference(east_wind, north_wind, pressure, sound_squared, column_mass, polar_rows, cutoffs):
    cosine, courant = latitude_terms(jnp.arange(NLAT, dtype=jnp.int32), NLAT)
    lat_factor = courant[None, :, None]
    blank = jnp.zeros((LEVELS, 1, NLON), pressure.dtype)
    east = jnp.roll(pressure, -1, axis=2)
    west = jnp.roll(pressure, 1, axis=2)
    north = jnp.concatenate([pressure[:, 1:], blank], axis=1)
    south = jnp.concatenate([blank, pressure[:, :-1]], axis=1)
    east_step = east_wind - lat_factor * (east - west) * 0.5
    north_step = north_wind - 0.3 * (north - south) * 0.5
    stacked = jnp.stack([east_step, north_step])
    chosen = stacked[:, :, polar_rows, :]
    spectrum = jnp.fft.fft(chosen, axis=-1)
    waves = jnp.arange(NLON, dtype=jnp.int32)
    waves = jnp.minimum(waves, NLON - waves)
    keeping = waves[None, :] <= cutoffs[:, None]
    spectrum = jnp.where(keeping[None, None], spectrum, jnp.zeros_like(spectrum))
    smoothed = jnp.real(jnp.fft.ifft(spectrum, axis=-1)).astype(pressure.dtype)
    updated = stacked.at[:, :, polar_rows, :].set(smoothed)
    new_east = updated[0]
    new_north = updated[1]
    carried = new_north * cosine[None, :, None]
    east_u = jnp.roll(new_east, -1, axis=2)
    west_u = jnp.roll(new_east, 1, axis=2)
    north_v = jnp.concatenate([carried[:, 1:], blank], axis=1)
    south_v = jnp.concatenate([blank, carried[:, :-1]], axis=1)
    divergence = lat_factor * (east_u - west_u) * 0.5 + 0.3 * (north_v - south_v) * 0.5 / cosine[None, :, None]
    new_pressure = pressure - sound_squared[:, None, None] * divergence / column_mass[None]
    return new_east, new_north, new_pressure
```

```python
import jax
import jax.numpy as jnp
from jax import lax
from jax.sharding import PartitionSpec as P

PRECISE = lax.Precision.HIGHEST
CLOSE = lax.Precision.HIGH


def shifted(shard, axis, dim, rim_zero):
    peers, length = (lax.axis_size(axis), shard.shape[dim])
    up = [(i, (i + 1) % peers) for i in range(peers)]
    down = [(j, i) for i, j in up]
    last = lax.slice_in_dim(shard, length - 1, length, axis=dim)
    first = lax.slice_in_dim(shard, 0, 1, axis=dim)
    before = lax.ppermute(last, axis, up)
    after = lax.ppermute(first, axis, down)
    if rim_zero:
        place = lax.axis_index(axis)
        before = jnp.where(place > 0, before, 0.0)
        after = jnp.where(place < peers - 1, after, 0.0)
    above = jnp.concatenate([lax.slice_in_dim(shard, 1, length, axis=dim), after], axis=dim)
    below = jnp.concatenate([before, lax.slice_in_dim(shard, 0, length - 1, axis=dim)], axis=dim)
    return above, below


def latitude_terms(global_rows, total_rows):
    latitude = (-0.5 + (global_rows.astype(jnp.float32) + 0.5) / total_rows) * jnp.pi
    cosine = jnp.cos(latitude)
    courant = 0.3 * jnp.minimum(1.0 / cosine, 2.0)
    return (cosine, courant)


def slot_table(polar_rows, cutoffs, band_number, row_count, slot_count):
    lower = band_number * row_count
    opening = jnp.sum((polar_rows < lower).astype(jnp.int32))
    closing = jnp.sum((polar_rows < lower + row_count).astype(jnp.int32))
    entries = opening + jnp.arange(slot_count, dtype=jnp.int32)
    present = entries < closing
    safe_entries = jnp.clip(entries, 0, polar_rows.shape[0] - 1)
    local_rows = jnp.clip(jnp.take(polar_rows, safe_entries) - lower, 0, row_count - 1)
    limits = jnp.take(cutoffs, safe_entries)
    return (present, local_rows, limits)


def dft_filter(row_data, limits):
    row_total, length = row_data.shape
    inner = 128
    outer = length // inner
    outer_ids = jnp.arange(outer, dtype=jnp.int32)
    inner_ids = jnp.arange(inner, dtype=jnp.int32)
    angle_one = (
        2.0 * jnp.pi * (outer_ids[:, None] * outer_ids[None, :] % outer).astype(jnp.float32) / outer
    )
    angle_two = (
        2.0 * jnp.pi * (inner_ids[:, None] * inner_ids[None, :] % inner).astype(jnp.float32) / inner
    )
    angle_twist = (
        2.0
        * jnp.pi
        * (outer_ids[:, None] * inner_ids[None, :] % length).astype(jnp.float32)
        / length
    )
    cos_one, sin_one = (jnp.cos(angle_one), jnp.sin(angle_one))
    cos_two, sin_two = (jnp.cos(angle_two), jnp.sin(angle_two))
    cos_twist, sin_twist = (jnp.cos(angle_twist), jnp.sin(angle_twist))
    folded = row_data.reshape(row_total, outer, inner)
    real_a = jnp.einsum("mab,ak->mkb", folded, cos_one, precision=CLOSE)
    imag_a = -jnp.einsum("mab,ak->mkb", folded, sin_one, precision=CLOSE)
    real_b = real_a * cos_twist + imag_a * sin_twist
    imag_b = imag_a * cos_twist - real_a * sin_twist
    real_c = jnp.einsum("mkb,bj->mkj", real_b, cos_two, precision=CLOSE) + jnp.einsum(
        "mkb,bj->mkj", imag_b, sin_two, precision=CLOSE
    )
    imag_c = jnp.einsum("mkb,bj->mkj", imag_b, cos_two, precision=CLOSE) - jnp.einsum(
        "mkb,bj->mkj", real_b, sin_two, precision=CLOSE
    )
    wave_ids = outer_ids[:, None] + outer * inner_ids[None, :]
    wave_ids = jnp.minimum(wave_ids, length - wave_ids)
    keeping = (wave_ids[None] <= limits[:, None, None]).astype(jnp.float32)
    real_c = real_c * keeping
    imag_c = imag_c * keeping
    real_d = jnp.einsum("mkj,jb->mkb", real_c, cos_two, precision=CLOSE) - jnp.einsum(
        "mkj,jb->mkb", imag_c, sin_two, precision=CLOSE
    )
    imag_d = jnp.einsum("mkj,jb->mkb", imag_c, cos_two, precision=CLOSE) + jnp.einsum(
        "mkj,jb->mkb", real_c, sin_two, precision=CLOSE
    )
    real_e = real_d * cos_twist - imag_d * sin_twist
    imag_e = imag_d * cos_twist + real_d * sin_twist
    result = jnp.einsum("mkb,ka->mab", real_e, cos_one, precision=CLOSE) - jnp.einsum(
        "mkb,ka->mab", imag_e, sin_one, precision=CLOSE
    )
    return (result / length).reshape(row_total, length)


def filter_round(items, slot_limits):
    slot_total = slot_limits.shape[0]
    whole_rows = lax.all_to_all(items, "lon", split_axis=0, concat_axis=1, tiled=True)
    share = whole_rows.shape[0]
    item_ids = lax.axis_index("lon") * share + jnp.arange(share, dtype=jnp.int32)
    item_limits = jnp.take(slot_limits, item_ids % slot_total)
    filtered = dft_filter(whole_rows, item_limits)
    return lax.all_to_all(filtered, "lon", split_axis=1, concat_axis=0, tiled=True)


def on_device(east_wind, north_wind, pressure, sound_squared, column_mass, polar_rows, cutoffs):
    level_count, row_count, seg_width = pressure.shape
    band_count = lax.axis_size("lat")
    band_number = lax.axis_index("lat")
    total_rows = row_count * band_count
    global_rows = band_number * row_count + jnp.arange(row_count, dtype=jnp.int32)
    cosine, courant = latitude_terms(global_rows, total_rows)
    lat_factor = courant[None, :, None]
    east, west = shifted(pressure, "lon", 2, False)
    north, south = shifted(pressure, "lat", 1, True)
    east_step = east_wind - lat_factor * (east - west) * 0.5
    north_step = north_wind - 0.3 * (north - south) * 0.5
    stacked = jnp.concatenate([east_step, north_step])
    slot_count = row_count // 2
    present, local_rows, limits = slot_table(
        polar_rows, cutoffs, band_number, row_count, slot_count
    )
    rows = jnp.arange(row_count, dtype=jnp.int32)
    hits = present[:, None] & (local_rows[:, None] == rows[None, :])
    one_hot = hits.astype(jnp.float32)
    listed = jnp.any(hits, axis=0)
    picked = jnp.einsum("sr,qrc->qsc", one_hot, stacked, precision=PRECISE)
    whole_limit = seg_width * lax.axis_size("lon") // 2
    smoothed = filter_round(
        picked.reshape(-1, seg_width), jnp.where(present, limits, whole_limit)
    ).reshape(picked.shape)
    spread = jnp.einsum("sr,qsc->qrc", one_hot, smoothed, precision=PRECISE)
    updated = jnp.where(listed[None, :, None], spread, stacked)
    new_east = updated[:level_count]
    new_north = updated[level_count:]
    east_u, west_u = shifted(new_east, "lon", 2, False)
    north_v, south_v = shifted(new_north * cosine[None, :, None], "lat", 1, True)
    divergence = (
        lat_factor * (east_u - west_u) * 0.5
        + 0.3 * (north_v - south_v) * 0.5 / cosine[None, :, None]
    )
    new_pressure = pressure - sound_squared[:, None, None] * divergence / column_mass[None]
    return (new_east, new_north, new_pressure)


def solution(mesh):
    in_specs = (
        P(None, "lat", "lon"),
        P(None, "lat", "lon"),
        P(None, "lat", "lon"),
        P(),
        P("lat", "lon"),
        P(),
        P(),
    )
    out_specs = (P(None, "lat", "lon"), P(None, "lat", "lon"), P(None, "lat", "lon"))
    return jax.shard_map(
        on_device, mesh=mesh, in_specs=in_specs, out_specs=out_specs, check_vma=False
    )
```
